256 devices in a mesh: ka: 4 (over x), pair: 16 (over z, core), aux: 4 (over y).
Axes of the slice: x: 4, y: 4, z: 8, core: 2. Of those that a mesh axis runs over, the one named last changes fastest.
Arguments:
- kpoint_grid: int32 [16, 3], P(('ka', 'aux')), may hold values from 0 to 3, as said below
- image_shift: int32 [3, 4, 6144], P(None, None, 'pair'), may hold values from -2 to 2
- density_k: bfloat16 [16, 4, 6144, 2, 1024], P(('ka', 'aux'), None, 'pair'), may hold values from -24 to 24
- coefficients: bfloat16 [2048, 256, 1024], P(('ka', 'pair'), 'aux'), may hold values from -1 to 1
- coulomb: float32 [24576, 256], P(('ka', 'pair'), 'aux'), may hold values from 0.002 to 0.08
- send_rows: int32 [64, 64, 32], P(('ka', 'pair')), may hold values from -1 to 383, as said below
- source_index: int32 [24576, 16], P(('ka', 'pair')), may hold values from 0 to 2431
- list_length: int32 [24576], P(('ka', 'pair')), may hold values from 1 to 16
Outputs:
- exchange_blocks: bfloat16 [24576, 1024], P(('ka', 'pair'), 'aux')
The draws below stay inside these ranges and needn't reach their ends.
Inputs may be any that keep to these rules, and one draw needn't show every extreme that they name: `kpoint_grid`: the rows are the 16 points of the 4 x 2 x 2 grid, each once, in an order drawn from the seed. `send_rows`: each entry is a row of the sending slab (below 384) or -1 for an empty slot; filled slots come first; each slab fills all 32 slots to the slab after it, cyclically.
All inputs are finite; a program needn't handle non-finite values.
Results may differ from the reference program's by a relative error of at most 0.025.
Values may be sent and summed in bfloat16 or wider, within the bound.
No kernel may reach another device: no remote copies, remote signals or barrier semaphores. Data moves between devices by JAX's collectives and lax.ppermute only.
A program may use at most 128 MiB of HBM per device.

```python
import math
import jax
import jax.numpy as jnp
from jax import lax

NB = 32
NAUX = 256
NK = 16
ATOM_DEV = 32
PAIRS_ATOM = 12
LIST = 16
CAP = 32
TP = 384
SLABS = 64
PAIRS = 24576
N_KA = 4
N_PAIR = 16


def draw_kpoint_grid(key, part):
    key = jax.random.fold_in(key, 5)
    order = jax.random.permutation(key, NK)
    return jnp.stack([order // 4, jnp.mod(order // 2, 2), jnp.mod(order, 2)], axis=1).astype(jnp.int32)


def draw_send_rows(key, part):
    key = jax.random.fold_in(key, 11)
    count_key, row_key = jax.random.split(key)
    counts = jax.random.randint(count_key, (SLABS, SLABS), 0, CAP + 1)
    after = jnp.mod(jnp.arange(SLABS) + 1, SLABS)
    full = jnp.arange(SLABS)[None, :] == after[:, None]
    counts = jnp.where(full, CAP, counts)
    rows = jax.random.randint(row_key, (SLABS, SLABS, CAP), 0, ATOM_DEV * PAIRS_ATOM)
    filled = jnp.arange(CAP)[None, None, :] < counts[:, :, None]
    return jnp.where(filled, rows, -1).astype(jnp.int32)


def touch_ends(array, stream_key, least, largest):
    extent = array.shape
    place = [jax.random.randint(jax.random.fold_in(stream_key, axis), (), 0, extent[axis]) for axis in range(len(extent))]
    array = array.at[tuple(place)].set(least)
    longest = extent.index(max(extent))
    place[longest] = (place[longest] + 1) % extent[longest]
    return array.at[tuple(place)].set(largest)


def block_scale(own_key, shape, pieces, least, high):
    def one(position, parts):
        heights = jax.random.uniform(jax.random.fold_in(jax.random.fold_in(own_key, 6), position), (parts,), jnp.float32, least / len(pieces), high / len(pieces))
        return jnp.repeat(jnp.exp(heights), shape[position] // parts).reshape((-1,) + (1,) * (len(shape) - position - 1))

    factor_of = one(*pieces[0])
    for cut in pieces[1:]:
        factor_of = factor_of * one(*cut)
    return factor_of


def gaussian(rng, dims, width, bound, cuts=(), kind=jnp.bfloat16):
    factor_of = block_scale(rng, dims, cuts, -0.22, 0.18) if cuts else 1.0
    entries = jax.random.normal(rng, dims, jnp.float32) * width * factor_of
    return jnp.minimum(jnp.maximum(entries, -bound), bound).astype(kind)


def setup_inputs(seed: int = 0) -> dict:
    key_of = jax.random.split(jax.random.key(seed), 9)
    return {
        "kpoint_grid": draw_kpoint_grid(jax.random.fold_in(key_of[8], 71), 0),
        "image_shift": touch_ends(jax.random.randint(key_of[1], (3, N_KA, N_PAIR * TP), -2, 3), jax.random.fold_in(key_of[1], 1), -2, 2).astype(jnp.int32),
        "density_k": gaussian(key_of[2], (NK, N_KA, N_PAIR * TP, 2, NB * NB), 4.0, 24.0, ((0, 16), (2, 16))),
        "coefficients": gaussian(key_of[3], (SLABS * ATOM_DEV, NAUX, NB * NB), NB ** -0.5, 1.0, ((0, 64), (1, 4))),
        "coulomb": jnp.clip(jnp.exp(math.log(0.08) - 3.6888794 * jax.random.uniform(key_of[4], (PAIRS, NAUX), jnp.float32) ** block_scale(key_of[4], (PAIRS, NAUX), ((0, 64), (1, 4)), -0.2, 0.2)), 0.002, 0.08),
        "send_rows": draw_send_rows(jax.random.fold_in(key_of[8], 71), 0),
        "source_index": touch_ends(jax.random.randint(key_of[6], (PAIRS, LIST), 0, TP + SLABS * CAP), jax.random.fold_in(key_of[6], 1), 0, (TP + SLABS * CAP) - 1).astype(jnp.int32),
        "list_length": touch_ends(jax.random.randint(key_of[7], (PAIRS,), 1, LIST + 1), jax.random.fold_in(key_of[7], 1), 1, LIST).astype(jnp.int32),
    }


def image_sum_all(kpoint_grid, image_shift, density_k):
    shifts = image_shift.reshape(3, -1)
    count = shifts.shape[1]
    blocks = density_k.reshape(NK, count, 2, NB * NB)

    def add_point(total, index):
        kvec = kpoint_grid[index]
        turns = jnp.mod(kvec[0] * shifts[0] * (NK // 4) + kvec[1] * shifts[1] * (NK // 2) + kvec[2] * shifts[2] * (NK // 2), NK)
        angle = turns.astype(jnp.float32) * (2.0 * math.pi / NK)
        block = blocks[index].astype(jnp.float32)
        term = (block[:, 0] * jnp.cos(angle)[:, None] + block[:, 1] * jnp.sin(angle)[:, None]) / NK
        term = lax.optimization_barrier(term.astype(jnp.bfloat16)).astype(jnp.float32)
        return total + term, None

    total, _ = lax.scan(add_point, jnp.zeros((count, NB * NB), jnp.float32), jnp.arange(NK))
    return total


def atom_block(items):
    coeff, ymat, weights = items
    coeff = coeff.reshape(NAUX, NB, NB).astype(jnp.float32)
    inner = jnp.einsum('pmn,tnl->tpml', coeff, ymat.astype(jnp.float32))
    inner = (inner * weights[:, :, None, None]).astype(jnp.bfloat16)
    return jnp.einsum('tpml,pkl->tmk', inner.astype(jnp.float32), coeff)


def reference(kpoint_grid, image_shift, density_k, coefficients, coulomb, send_rows, source_index, list_length):
    target_rows = ATOM_DEV * PAIRS_ATOM
    density = image_sum_all(kpoint_grid, image_shift, density_k).astype(jnp.bfloat16)
    density = density.reshape(SLABS, target_rows, NB * NB)
    incoming = jnp.transpose(send_rows, (1, 0, 2))
    slab_ids = jnp.arange(SLABS).astype(jnp.int32)

    def one_slab(items):
        slab_id, rows, sources, lengths, coeff, weights = items
        picked = density[slab_ids[:, None], jnp.maximum(rows, 0)]
        picked = jnp.where((rows >= 0)[..., None], picked, jnp.zeros((), jnp.bfloat16))
        pool = jnp.concatenate([density[slab_id], picked.reshape(SLABS * CAP, NB * NB)], 0)
        mask = (jnp.arange(LIST)[None, :] < lengths[:, None]).astype(jnp.float32)
        summed = jnp.einsum('tg,tgn->tn', mask, pool[sources].astype(jnp.float32)).astype(jnp.bfloat16)
        ymat = summed.reshape(ATOM_DEV, PAIRS_ATOM, NB, NB)
        result = lax.map(atom_block, (coeff, ymat, weights))
        return result.reshape(target_rows, NB * NB)

    blocks = lax.map(one_slab, (slab_ids, incoming,
                                source_index.reshape(SLABS, target_rows, LIST),
                                list_length.reshape(SLABS, target_rows),
                                coefficients.reshape(SLABS, ATOM_DEV, NAUX, NB * NB),
                                coulomb.reshape(SLABS, ATOM_DEV, PAIRS_ATOM, NAUX)))
    return blocks.reshape(SLABS * target_rows, NB * NB).astype(jnp.bfloat16)
```

```python
import math

import jax
import jax.numpy as jnp
from jax import lax
from jax.experimental import pallas as pl
from jax.experimental.pallas import tpu as pltpu
from jax.sharding import PartitionSpec as P

NB = 32
NK = 16
WIDE = 256
ROWS = 128
GROUP = 4
F32 = jnp.float32
BF16 = jnp.bfloat16
NT = (((1,), (1,)), ((), ()))
TN = (((0,), (0,)), ((), ()))


def iota(shape, dim):
    return lax.broadcasted_iota(jnp.int32, shape, dim)


def term_kernel(kp_ref, shift_ref, x_ref, o_ref):
    turns = (
        kp_ref[0, 0] * (NK // 4) * shift_ref[0, 0]
        + kp_ref[0, 1] * (NK // 2) * shift_ref[1, 0]
        + kp_ref[0, 2] * (NK // 2) * shift_ref[2, 0]
    ) & (NK - 1)
    angle = turns.astype(F32) * (2.0 * math.pi / NK)
    row, col = iota((2 * ROWS, ROWS), 0), iota((2 * ROWS, ROWS), 1)
    phase = jnp.where(
        row == 2 * col, jnp.cos(angle) / NK, jnp.where(row == 2 * col + 1, jnp.sin(angle) / NK, 0.0)
    )
    high = phase.astype(BF16)
    low = (phase - high.astype(F32)).astype(BF16)
    block = x_ref[...].reshape(2 * ROWS, x_ref.shape[-1])
    term = lax.dot_general(high, block, TN, preferred_element_type=F32)
    term += lax.dot_general(low, block, TN, preferred_element_type=F32)
    term = term.astype(BF16)
    for j in range(o_ref.shape[1]):
        o_ref[0, j] = term[:, WIDE * j : WIDE * (j + 1)]


def kpoint_terms(kpoint, shift, block):
    slabs, rows = block.shape[:2]
    width = block.shape[-1]
    steps = rows // ROWS
    return pl.pallas_call(
        term_kernel,
        grid=(slabs, steps),
        in_specs=[
            pl.BlockSpec(memory_space=pltpu.SMEM),
            pl.BlockSpec((3, 1, 1, ROWS), lambda g, i: (0, g, 0, i)),
            pl.BlockSpec((ROWS, 2, width), lambda g, i: (g * steps + i, 0, 0)),
        ],
        out_specs=pl.BlockSpec((1, width // WIDE, ROWS, WIDE), lambda g, i: (g, 0, i, 0)),
        out_shape=jax.ShapeDtypeStruct((slabs, width // WIDE, rows, WIDE), BF16),
    )(kpoint, shift.reshape(3, slabs, 1, rows), block.reshape(slabs * rows, 2, width))


def count_kernel(src_ref, len_ref, s_ref):
    rows, pool = s_ref.shape
    lane = iota((rows, pool), 1)
    total = jnp.zeros((rows, pool), F32)
    for g in range(src_ref.shape[1]):
        index = jnp.where(g < len_ref[...], src_ref[:, g : g + 1], -1)
        total += jnp.where(lane == index, 1.0, 0.0)
    s_ref[...] = total.astype(BF16)


def entry_counts(source_index, list_length, pool):
    targets, entries = source_index.shape
    step = 64
    return pl.pallas_call(
        count_kernel,
        grid=(targets // step,),
        in_specs=[
            pl.BlockSpec((step, entries), lambda i: (i, 0)),
            pl.BlockSpec((step, 1), lambda i: (i, 0)),
        ],
        out_specs=pl.BlockSpec((step, pool), lambda i: (i, 0)),
        out_shape=jax.ShapeDtypeStruct((targets, pool), BF16),
    )(source_index, list_length[:, None])


def pick_kernel(terms_ref, rows_ref, slab_ref, sent_ref):
    total = terms_ref[0].astype(F32)
    for k in range(1, terms_ref.shape[0]):
        total += terms_ref[k].astype(F32)
    slab = total.astype(BF16)
    slab_ref[...] = slab
    step = 256
    for i in range(sent_ref.shape[0] // step):
        rows = rows_ref[i * step : (i + 1) * step]
        hot = (rows == iota((step, slab.shape[0]), 1)).astype(F32).astype(BF16)
        sent_ref[i * step : (i + 1) * step] = jnp.dot(
            hot, slab, preferred_element_type=F32
        ).astype(BF16)


def pick(terms, rows):
    return pl.pallas_call(
        pick_kernel,
        out_shape=(
            jax.ShapeDtypeStruct(terms.shape[1:], BF16),
            jax.ShapeDtypeStruct((rows.shape[0], terms.shape[2]), BF16),
        ),
        compiler_params=pltpu.CompilerParams(vmem_limit_bytes=40 * 2**20),
    )(terms, rows)


def list_kernel(counts_ref, slab_ref, got_ref, y_ref):
    own = slab_ref.shape[0]
    total = jnp.dot(counts_ref[:, :own], slab_ref[...], preferred_element_type=F32)
    total += jnp.dot(counts_ref[:, own:], got_ref[...], preferred_element_type=F32)
    y_ref[...] = total.astype(BF16)


def list_sums(counts, slab, got):
    return pl.pallas_call(
        list_kernel,
        out_shape=jax.ShapeDtypeStruct((counts.shape[0], slab.shape[1]), BF16),
        compiler_params=pltpu.CompilerParams(vmem_limit_bytes=40 * 2**20),
    )(counts, slab, got)


def exchange_kernel(pairs_atom, c_ref, y_ref, w_ref, o_ref, y_rows, weighted, folded, gather, diag):
    atoms = c_ref.shape[0]
    targets = atoms * pairs_atom
    quarters = y_ref.shape[0]

    @pl.when(pl.program_id(0) == 0)
    def _():
        shape = (quarters * targets, targets * NB)
        row, col = iota(shape, 0), iota(shape, 1)
        keep = (row % targets == col // NB) & (row // targets == (col % NB) // 8)
        gather[...] = keep.astype(F32).astype(BF16)
        square = (WIDE, WIDE)
        diag[...] = (iota(square, 0) // NB == iota(square, 1) // NB).astype(F32).astype(BF16)

    square = (WIDE, WIDE)
    fold = (iota(square, 0) % NB == iota(square, 1) % NB).astype(F32).astype(BF16)
    spread = (targets, 8, WIDE)
    keep = iota(spread, 2) // NB == iota(spread, 1)
    parts = []
    for j in range(quarters):
        y = y_ref[j].astype(F32)
        parts.append(jnp.where(keep, jnp.broadcast_to(y[:, None, :], spread), 0.0))
    rows = jnp.concatenate(parts, axis=1).reshape(targets * NB, WIDE).astype(BF16)
    y_rows[...] = jnp.dot(rows, fold, preferred_element_type=F32).astype(BF16)
    tall = (pairs_atom * NB, WIDE)
    keep_out = iota(tall, 0) % 8 == iota(tall, 1) // NB

    def atom(a, carry):
        c = c_ref[a]
        for t in range(pairs_atom):
            target = a * pairs_atom + t
            y = y_rows[pl.ds(pl.multiple_of(target * NB, NB), NB), :]
            y = jnp.concatenate([y] * 8, axis=0) * diag[...]
            inner = jnp.dot(c, y, preferred_element_type=F32)
            inner = inner.reshape(8, NB, WIDE) * w_ref[target][:, None, :]
            inner = inner.astype(BF16)
            for p in range(8):
                weighted[p, t * NB : (t + 1) * NB, :] = inner[p]
        total = jnp.zeros(tall, F32)
        for p in range(8):
            copies = jnp.concatenate([c[NB * p : NB * (p + 1), :]] * 8, axis=0)
            total += lax.dot_general(weighted[p], copies, NT, preferred_element_type=F32)
        start = pl.multiple_of(a * pairs_atom * NB, 128)
        folded[pl.ds(start, pairs_atom * NB), :] = jnp.where(keep_out, total, 0.0).astype(BF16)
        return carry

    lax.fori_loop(0, atoms, atom, 0)
    result = jnp.dot(gather[...], folded[...], preferred_element_type=F32).astype(BF16)
    for j in range(quarters):
        o_ref[j] = result[j * targets : (j + 1) * targets]


def exchange(coeff, y, weights):
    atoms = coeff.shape[0]
    quarters, targets = y.shape[:2]
    pairs_atom = targets // atoms
    step = GROUP * pairs_atom

    def kernel(*refs):
        exchange_kernel(pairs_atom, *refs)

    return pl.pallas_call(
        kernel,
        grid=(atoms // GROUP,),
        in_specs=[
            pl.BlockSpec((GROUP, WIDE, WIDE), lambda i: (i, 0, 0)),
            pl.BlockSpec((quarters, step, WIDE), lambda i: (0, i, 0)),
            pl.BlockSpec((step, 8, WIDE), lambda i: (i, 0, 0)),
        ],
        out_specs=pl.BlockSpec((quarters, step, WIDE), lambda i: (0, i, 0)),
        out_shape=jax.ShapeDtypeStruct((quarters, targets, WIDE), BF16),
        scratch_shapes=[
            pltpu.VMEM((step * NB, WIDE), BF16),
            pltpu.VMEM((8, pairs_atom * NB, WIDE), BF16),
            pltpu.VMEM((step * NB, WIDE), BF16),
            pltpu.VMEM((quarters * step, step * NB), BF16),
            pltpu.VMEM((WIDE, WIDE), BF16),
        ],
        compiler_params=pltpu.CompilerParams(vmem_limit_bytes=40 * 2**20),
    )(coeff, y, weights)


def shards(
    kpoint_grid, image_shift, density_k, coefficients, coulomb, send_rows, source_index, list_length
):
    atoms, aux_local = coefficients.shape[:2]
    targets = coulomb.shape[0]
    coeff = coefficients.reshape(atoms, 8, 8, NB, NB)
    coeff = coeff.transpose(0, 1, 3, 2, 4).reshape(atoms, WIDE, WIDE)
    weights = jnp.repeat(coulomb, NB, axis=1).reshape(targets, 8, WIDE)
    slots = send_rows.shape[1] * send_rows.shape[2]
    counts = entry_counts(source_index, list_length, targets + slots)
    rows_out = send_rows.reshape(slots, 1)

    terms = kpoint_terms(kpoint_grid, image_shift, density_k[0])
    terms = terms.reshape(NK, targets, WIDE)
    terms = lax.all_to_all(terms, ("ka", "aux"), split_axis=0, concat_axis=0, tiled=True)
    slab, sent = pick(terms, rows_out)
    sent = sent.reshape(send_rows.shape[1], send_rows.shape[2], WIDE)
    got = lax.all_to_all(sent, ("ka", "pair"), split_axis=0, concat_axis=0, tiled=True)
    y = list_sums(counts, slab, got.reshape(slots, WIDE))
    y = lax.all_gather(y, "aux")
    partial = exchange(coeff, y, weights)
    parts = lax.all_to_all(partial, "aux", split_axis=0, concat_axis=0, tiled=True)
    return jnp.sum(parts.astype(F32), axis=0).astype(BF16)


def solution(mesh):
    placed = (
        P(("ka", "aux"), None),
        P(None, None, "pair"),
        P(("ka", "aux"), None, "pair", None, None),
        P(("ka", "pair"), "aux", None),
        P(("ka", "pair"), "aux"),
        P(("ka", "pair"), None, None),
        P(("ka", "pair"), None),
        P(("ka", "pair")),
    )
    return jax.shard_map(
        shards, mesh=mesh, in_specs=placed, out_specs=P(("ka", "pair"), "aux"), check_vma=False
    )
```

```python
import math

import jax
import jax.numpy as jnp
from jax import lax
from jax.experimental import pallas as pl
from jax.experimental.pallas import tpu as pltpu
from jax.sharding import PartitionSpec as P

NB = 32
NK = 16
WIDE = 256
ROWS = 128
GROUP = 4
QUARTERS = 4
AXES = ("ka", "pair", "aux")
F32 = jnp.float32
BF16 = jnp.bfloat16
NT = (((1,), (1,)), ((), ()))
TN = (((0,), (0,)), ((), ()))


def iota(shape, dim):
    return lax.broadcasted_iota(jnp.int32, shape, dim)


def term_kernel(kp_ref, me_ref, shift_ref, x_ref, o_ref):
    g = pl.program_id(0)
    rows, _, width = x_ref.shape
    turns = (
        kp_ref[0, 0] * (NK // 4) * shift_ref[0, 0]
        + kp_ref[0, 1] * (NK // 2) * shift_ref[1, 0]
        + kp_ref[0, 2] * (NK // 2) * shift_ref[2, 0]
    ) & (NK - 1)
    angle = turns.astype(F32) * (2.0 * math.pi / NK)
    even, odd = jnp.cos(angle) / NK, jnp.sin(angle) / NK
    row, col = iota((2 * ROWS, ROWS), 0), iota((2 * ROWS, ROWS), 1)
    core, second = me_ref[0], me_ref[1]
    for i in range(rows // ROWS):
        here = slice(i * ROWS, (i + 1) * ROWS)
        phase = jnp.where(
            row == 2 * col, even[:, here], jnp.where(row == 2 * col + 1, odd[:, here], 0.0)
        )
        high = phase.astype(BF16)
        low = (phase - high.astype(F32)).astype(BF16)
        both = jnp.concatenate([high, low], axis=1).T
        block = x_ref[here].reshape(2 * ROWS, width)
        term = jnp.dot(both, block, preferred_element_type=F32)
        term = (term[:ROWS] + term[ROWS:]).astype(BF16)
        for j in range(width // WIDE):
            first = jnp.where(core == 0, g, j)
            other = (jnp.where(core == 0, j, g) - second) & 3
            o_ref[first, other, here] = term[:, WIDE * j : WIDE * (j + 1)]


def kpoint_terms(kpoint, me, shift, block):
    slabs, rows = block.shape[:2]
    width = block.shape[-1]
    shape = (slabs, width // WIDE, rows, WIDE)
    return pl.pallas_call(
        term_kernel,
        grid=(slabs,),
        in_specs=[
            pl.BlockSpec(memory_space=pltpu.SMEM),
            pl.BlockSpec(memory_space=pltpu.SMEM),
            pl.BlockSpec((3, 1, 1, rows), lambda g: (0, g, 0, 0)),
            pl.BlockSpec((rows, 2, width), lambda g: (g, 0, 0)),
        ],
        out_specs=pl.BlockSpec(shape, lambda g: (0, 0, 0, 0)),
        out_shape=jax.ShapeDtypeStruct(shape, BF16),
        compiler_params=pltpu.CompilerParams(vmem_limit_bytes=40 * 2**20),
    )(kpoint, me, shift.reshape(3, slabs, 1, rows), block.reshape(slabs * rows, 2, width))


def half_sum_kernel(x_ref, *o_refs):
    for q, o_ref in enumerate(o_refs):
        total = x_ref[0, q].astype(F32)
        for f in range(1, x_ref.shape[0]):
            total += x_ref[f, q].astype(F32)
        o_ref[...] = total.astype(BF16)


def half_sums(terms):
    parts, others, rows, width = terms.shape
    step = rows // 3
    return pl.pallas_call(
        half_sum_kernel,
        grid=(rows // step,),
        in_specs=[pl.BlockSpec((parts, others, step, width), lambda i: (0, 0, i, 0))],
        out_specs=[pl.BlockSpec((step, width), lambda i: (i, 0))] * others,
        out_shape=[jax.ShapeDtypeStruct((rows, width), BF16)] * others,
        compiler_params=pltpu.CompilerParams(vmem_limit_bytes=40 * 2**20),
    )(terms)


def relay_kernel(x_ref, o_ref, wide, place):
    @pl.when(pl.program_id(0) == 0)
    def _():
        row, col = iota((WIDE, WIDE), 0), iota((WIDE, WIDE), 1)
        for p in range(8):
            keep = (row % NB == col % NB) & (col // NB == p)
            place[p] = keep.astype(F32).astype(BF16)

    wide[...] = x_ref[0].astype(F32)
    keep = iota((8, WIDE), 0) == iota((8, WIDE), 1) // NB
    total = jnp.zeros((WIDE, WIDE), F32)
    for p in range(8):
        rows = []
        for q in range(8):
            for j in range(4):
                row = wide[8 * q + p : 8 * q + p + 1, WIDE * j : WIDE * (j + 1)]
                rows.append(jnp.where(keep, jnp.broadcast_to(row, (8, WIDE)), 0.0))
        rows = jnp.concatenate(rows, axis=0).astype(BF16)
        total += jnp.dot(rows, place[p], preferred_element_type=F32)
    o_ref[0] = total.astype(BF16)


def relay_coefficients(coefficients):
    atoms, aux, width = coefficients.shape
    return pl.pallas_call(
        relay_kernel,
        grid=(atoms,),
        in_specs=[pl.BlockSpec((1, aux, width), lambda i: (i, 0, 0))],
        out_specs=pl.BlockSpec((1, WIDE, WIDE), lambda i: (i, 0, 0)),
        out_shape=jax.ShapeDtypeStruct((atoms, WIDE, WIDE), BF16),
        scratch_shapes=[pltpu.VMEM((aux, width), F32), pltpu.VMEM((8, WIDE, WIDE), BF16)],
    )(coefficients)


def count_kernel(src_ref, len_ref, coul_ref, s_ref, w_ref):
    coul = coul_ref[...]
    rows, aux = coul.shape
    high = coul.astype(BF16)
    rest = coul - high.astype(F32)
    middle = rest.astype(BF16)
    pieces = [high, middle, (rest - middle.astype(F32)).astype(BF16)]
    for p in range(aux // 8):
        keep = iota((aux, WIDE), 0) == 8 * p + iota((aux, WIDE), 1) // NB
        keep = keep.astype(F32).astype(BF16)
        spread = [jnp.dot(piece, keep, preferred_element_type=F32) for piece in pieces]
        w_ref[:, p, :] = (spread[0] + spread[1]) + spread[2]
    rows, pool = s_ref.shape
    lane = iota((rows, pool), 1)
    total = jnp.zeros((rows, pool), F32)
    for g in range(src_ref.shape[1]):
        index = jnp.where(g < len_ref[...], src_ref[:, g : g + 1], -1)
        total += jnp.where(lane == index, 1.0, 0.0)
    s_ref[...] = total.astype(BF16)


def entry_counts(source_index, list_length, coulomb, pool):
    targets, entries = source_index.shape
    aux = coulomb.shape[1]
    step = 64
    return pl.pallas_call(
        count_kernel,
        grid=(targets // step,),
        in_specs=[
            pl.BlockSpec((step, entries), lambda i: (i, 0)),
            pl.BlockSpec((step, 1), lambda i: (i, 0)),
            pl.BlockSpec((step, aux), lambda i: (i, 0)),
        ],
        out_specs=[
            pl.BlockSpec((step, pool), lambda i: (i, 0)),
            pl.BlockSpec((step, aux // 8, WIDE), lambda i: (i, 0, 0)),
        ],
        out_shape=[
            jax.ShapeDtypeStruct((targets, pool), BF16),
            jax.ShapeDtypeStruct((targets, aux // 8, WIDE), F32),
        ],
    )(source_index, list_length[:, None], coulomb)


def pick_kernel(rows_ref, own_ref, a_ref, b_ref, c_ref, slab_ref, sent_ref):
    total = own_ref[...].astype(F32) + a_ref[...].astype(F32)
    total += b_ref[...].astype(F32) + c_ref[...].astype(F32)
    slab = total.astype(BF16)
    slab_ref[...] = slab
    step = 256
    for i in range(sent_ref.shape[0] // step):
        rows = rows_ref[i * step : (i + 1) * step]
        hot = (rows == iota((step, slab.shape[0]), 1)).astype(F32).astype(BF16)
        sent_ref[i * step : (i + 1) * step] = jnp.dot(
            hot, slab, preferred_element_type=F32
        ).astype(BF16)


def pick(rows, parts):
    shape = parts[0].shape
    return pl.pallas_call(
        pick_kernel,
        out_shape=(
            jax.ShapeDtypeStruct(shape, BF16),
            jax.ShapeDtypeStruct((rows.shape[0], shape[1]), BF16),
        ),
        compiler_params=pltpu.CompilerParams(vmem_limit_bytes=40 * 2**20),
    )(rows, *parts)


def list_kernel(counts_ref, slab_ref, got_ref, y_ref):
    own = slab_ref.shape[0]
    total = jnp.dot(counts_ref[:, :own], slab_ref[...], preferred_element_type=F32)
    total += jnp.dot(counts_ref[:, own:], got_ref[...], preferred_element_type=F32)
    y_ref[...] = total.astype(BF16)


def list_sums(counts, slab, got):
    return pl.pallas_call(
        list_kernel,
        out_shape=jax.ShapeDtypeStruct((counts.shape[0], slab.shape[1]), BF16),
        compiler_params=pltpu.CompilerParams(vmem_limit_bytes=40 * 2**20),
    )(counts, slab, got)


def exchange_kernel(pairs_atom, me_ref, c_ref, w_ref, *refs):
    y_refs, o_refs = refs[:QUARTERS], refs[QUARTERS : 2 * QUARTERS]
    y_all, y_rows, weighted, folded, gather, diag = refs[2 * QUARTERS :]
    atoms = c_ref.shape[0]
    targets = atoms * pairs_atom
    me = me_ref[0]

    @pl.when(pl.program_id(0) == 0)
    def _():
        shape = (QUARTERS * targets, targets * NB)
        row, col = iota(shape, 0), iota(shape, 1)
        quarter = (row // targets + me) & 3
        keep = (row % targets == col // NB) & (quarter == (col % NB) // 8)
        gather[...] = keep.astype(F32).astype(BF16)
        square = (WIDE, WIDE)
        diag[...] = (iota(square, 0) // NB == iota(square, 1) // NB).astype(F32).astype(BF16)

    square = (WIDE, WIDE)
    fold = (iota(square, 0) % NB == iota(square, 1) % NB).astype(F32).astype(BF16)
    spread = (targets, 8, WIDE)
    keep = iota(spread, 2) // NB == iota(spread, 1)
    for r, y_ref in enumerate(y_refs):
        y_all[(me + r) & 3] = y_ref[...].astype(F32)
    parts = []
    for j in range(QUARTERS):
        parts.append(jnp.where(keep, jnp.broadcast_to(y_all[j][:, None, :], spread), 0.0))
    rows = jnp.concatenate(parts, axis=1).reshape(targets * NB, WIDE).astype(BF16)
    y_rows[...] = jnp.dot(rows, fold, preferred_element_type=F32).astype(BF16)
    tall = (pairs_atom * NB, WIDE)
    keep_out = iota(tall, 0) % 8 == iota(tall, 1) // NB

    def atom(a, carry):
        c = c_ref[a]
        for t in range(pairs_atom):
            target = a * pairs_atom + t
            y = y_rows[pl.ds(pl.multiple_of(target * NB, NB), NB), :]
            y = jnp.concatenate([y] * 8, axis=0) * diag[...]
            inner = jnp.dot(c, y, preferred_element_type=F32)
            inner = inner.reshape(8, NB, WIDE) * w_ref[target][:, None, :]
            inner = inner.astype(BF16)
            for p in range(8):
                weighted[p, t * NB : (t + 1) * NB, :] = inner[p]
        total = jnp.zeros(tall, F32)
        for p in range(8):
            copies = jnp.concatenate([c[NB * p : NB * (p + 1), :]] * 8, axis=0)
            total += lax.dot_general(weighted[p], copies, NT, preferred_element_type=F32)
        start = pl.multiple_of(a * pairs_atom * NB, 128)
        folded[pl.ds(start, pairs_atom * NB), :] = jnp.where(keep_out, total, 0.0).astype(BF16)
        return carry

    lax.fori_loop(0, atoms, atom, 0)
    result = jnp.dot(gather[...], folded[...], preferred_element_type=F32).astype(BF16)
    for r, o_ref in enumerate(o_refs):
        o_ref[...] = result[r * targets : (r + 1) * targets]


def exchange(me, coeff, weights, quarters):
    atoms = coeff.shape[0]
    targets = weights.shape[0]
    pairs_atom = targets // atoms
    step = GROUP * pairs_atom
    part = pl.BlockSpec((step, WIDE), lambda i: (i, 0))

    def kernel(*refs):
        exchange_kernel(pairs_atom, *refs)

    return pl.pallas_call(
        kernel,
        grid=(atoms // GROUP,),
        in_specs=[
            pl.BlockSpec(memory_space=pltpu.SMEM),
            pl.BlockSpec((GROUP, WIDE, WIDE), lambda i: (i, 0, 0)),
            pl.BlockSpec((step, 8, WIDE), lambda i: (i, 0, 0)),
        ]
        + [part] * QUARTERS,
        out_specs=[part] * QUARTERS,
        out_shape=[jax.ShapeDtypeStruct((targets, WIDE), BF16)] * QUARTERS,
        scratch_shapes=[
            pltpu.VMEM((QUARTERS, step, WIDE), F32),
            pltpu.VMEM((step * NB, WIDE), BF16),
            pltpu.VMEM((8, pairs_atom * NB, WIDE), BF16),
            pltpu.VMEM((step * NB, WIDE), BF16),
            pltpu.VMEM((QUARTERS * step, step * NB), BF16),
            pltpu.VMEM((WIDE, WIDE), BF16),
        ],
        compiler_params=pltpu.CompilerParams(vmem_limit_bytes=40 * 2**20),
    )(me, coeff, weights, *quarters)


def rank(mesh, k, p, a):
    return (k % mesh.shape["ka"] * mesh.shape["pair"] + p) * mesh.shape["aux"] + a % mesh.shape["aux"]


def first_groups(mesh):
    ka, pair, aux = (mesh.shape[n] for n in AXES)
    groups = []
    for p in range(pair):
        if p % 2 == 0:
            groups += [[rank(mesh, k, p, a) for k in range(ka)] for a in range(aux)]
        else:
            groups += [[rank(mesh, k, p, a) for a in range(aux)] for k in range(ka)]
    return groups


def second_shift(mesh, by):
    ka, pair, aux = (mesh.shape[n] for n in AXES)
    pairs = []
    for k in range(ka):
        for p in range(pair):
            for a in range(aux):
                to = rank(mesh, k, p, a + by) if p % 2 == 0 else rank(mesh, k + by, p, a)
                pairs.append((rank(mesh, k, p, a), to))
    return pairs


def along_aux(array, by):
    return lax.ppermute(array, "aux", [(i, (i + by) % QUARTERS) for i in range(QUARTERS)])


def make_shards(mesh):
    def shards(
        kpoint_grid,
        image_shift,
        density_k,
        coefficients,
        coulomb,
        send_rows,
        source_index,
        list_length,
    ):
        targets = coulomb.shape[0]
        slots = send_rows.shape[1] * send_rows.shape[2]
        core = lax.axis_index("pair") % 2
        aux = lax.axis_index("aux")
        second = jnp.where(core == 0, aux, lax.axis_index("ka"))
        me = jnp.stack([core, second]).astype(jnp.int32)

        terms = kpoint_terms(kpoint_grid, me, image_shift, density_k[0])
        terms, coulomb, source_index, list_length, send_rows = lax.optimization_barrier(
            (terms, coulomb, source_index, list_length, send_rows)
        )
        terms = lax.all_to_all(
            terms, AXES, split_axis=0, concat_axis=0, tiled=True, axis_index_groups=first_groups(mesh)
        )
        counts, weights = entry_counts(source_index, list_length, coulomb, targets + slots)
        rows_out = send_rows.reshape(slots, 1)
        terms, weights, counts, rows_out = lax.optimization_barrier(
            (terms, weights, counts, rows_out)
        )
        halves = half_sums(terms)
        parts = [halves[0]] + [
            lax.ppermute(halves[by], AXES, second_shift(mesh, by)) for by in (2, 1, 3)
        ]
        slab, sent = pick(rows_out, parts)
        sent, coefficients = lax.optimization_barrier((sent, coefficients))
        sent = sent.reshape(send_rows.shape[1], send_rows.shape[2], WIDE)
        got = lax.all_to_all(sent, ("ka", "pair"), split_axis=0, concat_axis=0, tiled=True)
        coeff = relay_coefficients(coefficients)
        got, coeff = lax.optimization_barrier((got, coeff))
        y = list_sums(counts, slab, got.reshape(slots, WIDE))
        far, right, left = along_aux(y, 2), along_aux(y, -1), along_aux(y, 1)
        own, a, b, c = exchange(aux.reshape(1).astype(jnp.int32), coeff, weights, (y, right, far, left))
        total = own.astype(F32) + along_aux(b, 2).astype(F32)
        total += along_aux(a, 1).astype(F32) + along_aux(c, 3).astype(F32)
        return total.astype(BF16)

    return shards


def solution(mesh):
    placed = (
        P(("ka", "aux"), None),
        P(None, None, "pair"),
        P(("ka", "aux"), None, "pair", None, None),
        P(("ka", "pair"), "aux", None),
        P(("ka", "pair"), "aux"),
        P(("ka", "pair"), None, None),
        P(("ka", "pair"), None),
        P(("ka", "pair")),
    )
    return jax.shard_map(
        make_shards(mesh),
        mesh=mesh,
        in_specs=placed,
        out_specs=P(("ka", "pair"), "aux"),
        check_vma=False,
    )
```

```python
import math

import jax
import jax.numpy as jnp
from jax import lax
from jax.experimental import pallas as pl
from jax.experimental.pallas import tpu as pltpu
from jax.sharding import PartitionSpec as P

NB = 32
NK = 16
WIDE = 256
ROWS = 128
GROUP = 4
QUARTERS = 4
FULL = 60 * 2**20
AXES = ("ka", "pair", "aux")
F32 = jnp.float32
BF16 = jnp.bfloat16
NT = (((1,), (1,)), ((), ()))
TN = (((0,), (0,)), ((), ()))


def iota(shape, dim):
    return lax.broadcasted_iota(jnp.int32, shape, dim)


def term_kernel(kp_ref, shift_ref, x_ref, o_ref, stage, sem):
    g = pl.program_id(0)
    rows, _, width = x_ref.shape
    turns = (
        kp_ref[0, 0] * (NK // 4) * shift_ref[0, pl.ds(g, 1)]
        + kp_ref[0, 1] * (NK // 2) * shift_ref[1, pl.ds(g, 1)]
        + kp_ref[0, 2] * (NK // 2) * shift_ref[2, pl.ds(g, 1)]
    ) & (NK - 1)
    angle = turns.astype(F32) * (2.0 * math.pi / NK)
    even, odd = jnp.cos(angle) / NK, jnp.sin(angle) / NK
    row, col = iota((2 * ROWS, ROWS), 0), iota((2 * ROWS, ROWS), 1)
    core = lax.axis_index("pair") % 2
    second = jnp.where(core == 0, lax.axis_index("aux"), lax.axis_index("ka"))
    pieces = width // WIDE

    def copy_out(slab, j):
        first = jnp.where(core == 0, slab, j)
        other = (jnp.where(core == 0, j, slab) - second) & 3
        return pltpu.make_async_copy(stage.at[slab, j], o_ref.at[first, other], sem.at[slab, j])

    for i in range(rows // ROWS):
        here = slice(i * ROWS, (i + 1) * ROWS)
        phase = jnp.where(
            row == 2 * col, even[:, here], jnp.where(row == 2 * col + 1, odd[:, here], 0.0)
        )
        high = phase.astype(BF16)
        low = (phase - high.astype(F32)).astype(BF16)
        both = jnp.concatenate([high, low], axis=1).T
        block = x_ref[here].reshape(2 * ROWS, width)
        term = jnp.dot(both, block, preferred_element_type=F32)
        term = (term[:ROWS] + term[ROWS:]).astype(BF16)
        for j in range(pieces):
            stage[g, j, here] = term[:, WIDE * j : WIDE * (j + 1)]
    for j in range(pieces):
        copy_out(g, j).start()

    @pl.when(g == stage.shape[0] - 1)
    def _():
        for slab in range(stage.shape[0]):
            for j in range(pieces):
                copy_out(slab, j).wait()


def kpoint_terms(kpoint, shift, block):
    slabs, rows = block.shape[:2]
    width = block.shape[-1]
    shape = (slabs, width // WIDE, rows, WIDE)
    return pl.pallas_call(
        term_kernel,
        grid=(slabs,),
        in_specs=[
            pl.BlockSpec(memory_space=pltpu.SMEM),
            pl.BlockSpec((3, slabs, rows), lambda g: (0, 0, 0)),
            pl.BlockSpec((rows, 2, width), lambda g: (g, 0, 0)),
        ],
        out_specs=pl.BlockSpec(memory_space=pl.ANY),
        out_shape=jax.ShapeDtypeStruct(shape, BF16),
        scratch_shapes=[pltpu.VMEM(shape, BF16), pltpu.SemaphoreType.DMA(shape[:2])],
        compiler_params=pltpu.CompilerParams(vmem_limit_bytes=FULL),
    )(kpoint, shift, block.reshape(slabs * rows, 2, width))


def half_sum_kernel(x_ref, *o_refs):
    for q, o_ref in enumerate(o_refs):
        total = x_ref[0, q].astype(F32)
        for f in range(1, x_ref.shape[0]):
            total += x_ref[f, q].astype(F32)
        o_ref[...] = total.astype(BF16)


def half_sums(terms):
    parts, others, rows, width = terms.shape
    step = rows // 3
    return pl.pallas_call(
        half_sum_kernel,
        grid=(rows // step,),
        in_specs=[pl.BlockSpec((parts, others, step, width), lambda i: (0, 0, i, 0))],
        out_specs=[pl.BlockSpec((step, width), lambda i: (i, 0))] * others,
        out_shape=[jax.ShapeDtypeStruct((rows, width), BF16)] * others,
        compiler_params=pltpu.CompilerParams(vmem_limit_bytes=40 * 2**20),
    )(terms)


def relay_kernel(x_ref, o_ref, wide, place):
    @pl.when(pl.program_id(0) == 0)
    def _():
        row, col = iota((WIDE, WIDE), 0), iota((WIDE, WIDE), 1)
        for p in range(8):
            keep = (row % NB == col % NB) & (col // NB == p)
            place[p] = keep.astype(F32).astype(BF16)

    wide[...] = x_ref[0].astype(F32)
    keep = iota((8, WIDE), 0) == iota((8, WIDE), 1) // NB
    total = jnp.zeros((WIDE, WIDE), F32)
    for p in range(8):
        rows = []
        for q in range(8):
            for j in range(4):
                row = wide[8 * q + p : 8 * q + p + 1, WIDE * j : WIDE * (j + 1)]
                rows.append(jnp.where(keep, jnp.broadcast_to(row, (8, WIDE)), 0.0))
        rows = jnp.concatenate(rows, axis=0).astype(BF16)
        total += jnp.dot(rows, place[p], preferred_element_type=F32)
    o_ref[0] = total.astype(BF16)


def relay_coefficients(coefficients):
    atoms, aux, width = coefficients.shape
    return pl.pallas_call(
        relay_kernel,
        grid=(atoms,),
        in_specs=[pl.BlockSpec((1, aux, width), lambda i: (i, 0, 0))],
        out_specs=pl.BlockSpec((1, WIDE, WIDE), lambda i: (i, 0, 0)),
        out_shape=jax.ShapeDtypeStruct((atoms, WIDE, WIDE), BF16),
        scratch_shapes=[pltpu.VMEM((aux, width), F32), pltpu.VMEM((8, WIDE, WIDE), BF16)],
    )(coefficients)


def count_kernel(src_ref, len_ref, coul_ref, s_ref, w_ref):
    coul = coul_ref[...]
    rows, aux = coul.shape
    high = coul.astype(BF16)
    rest = coul - high.astype(F32)
    middle = rest.astype(BF16)
    pieces = [high, middle, (rest - middle.astype(F32)).astype(BF16)]
    for p in range(aux // 8):
        keep = iota((aux, WIDE), 0) == 8 * p + iota((aux, WIDE), 1) // NB
        keep = keep.astype(F32).astype(BF16)
        spread = [jnp.dot(piece, keep, preferred_element_type=F32) for piece in pieces]
        w_ref[:, p, :] = (spread[0] + spread[1]) + spread[2]
    rows, pool = s_ref.shape
    lane = iota((rows, pool), 1)
    total = jnp.zeros((rows, pool), F32)
    for g in range(src_ref.shape[1]):
        index = jnp.where(g < len_ref[...], src_ref[:, g : g + 1], -1)
        total += jnp.where(lane == index, 1.0, 0.0)
    s_ref[...] = total.astype(BF16)


def entry_counts(source_index, list_length, coulomb, pool):
    targets, entries = source_index.shape
    aux = coulomb.shape[1]
    step = 64
    return pl.pallas_call(
        count_kernel,
        grid=(targets // step,),
        in_specs=[
            pl.BlockSpec((step, entries), lambda i: (i, 0)),
            pl.BlockSpec((step, 1), lambda i: (i, 0)),
            pl.BlockSpec((step, aux), lambda i: (i, 0)),
        ],
        out_specs=[
            pl.BlockSpec((step, pool), lambda i: (i, 0)),
            pl.BlockSpec((step, aux // 8, WIDE), lambda i: (i, 0, 0)),
        ],
        out_shape=[
            jax.ShapeDtypeStruct((targets, pool), BF16),
            jax.ShapeDtypeStruct((targets, aux // 8, WIDE), F32),
        ],
    )(source_index, list_length[:, None], coulomb)


def pick_kernel(rows_ref, own_ref, a_ref, b_ref, c_ref, slab_ref, sent_ref):
    total = own_ref[...].astype(F32) + a_ref[...].astype(F32)
    total += b_ref[...].astype(F32) + c_ref[...].astype(F32)
    slab = total.astype(BF16)
    slab_ref[...] = slab
    step = 256
    for i in range(sent_ref.shape[0] // step):
        rows = rows_ref[i * step : (i + 1) * step]
        hot = (rows == iota((step, slab.shape[0]), 1)).astype(F32).astype(BF16)
        sent_ref[i * step : (i + 1) * step] = jnp.dot(
            hot, slab, preferred_element_type=F32
        ).astype(BF16)


def pick(rows, parts):
    shape = parts[0].shape
    return pl.pallas_call(
        pick_kernel,
        out_shape=(
            jax.ShapeDtypeStruct(shape, BF16),
            jax.ShapeDtypeStruct((rows.shape[0], shape[1]), BF16),
        ),
        compiler_params=pltpu.CompilerParams(vmem_limit_bytes=40 * 2**20),
    )(rows, *parts)


def list_kernel(counts_ref, slab_ref, got_ref, y_ref):
    own = slab_ref.shape[0]
    total = jnp.dot(counts_ref[:, :own], slab_ref[...], preferred_element_type=F32)
    total += jnp.dot(counts_ref[:, own:], got_ref[...], preferred_element_type=F32)
    y_ref[...] = total.astype(BF16)


def list_sums(counts, slab, got):
    return pl.pallas_call(
        list_kernel,
        out_shape=jax.ShapeDtypeStruct((counts.shape[0], slab.shape[1]), BF16),
        compiler_params=pltpu.CompilerParams(vmem_limit_bytes=40 * 2**20),
    )(counts, slab, got)


def exchange_kernel(pairs_atom, me_ref, c_ref, w_ref, *refs):
    y_refs, o_refs = refs[:QUARTERS], refs[QUARTERS : 2 * QUARTERS]
    y_all, y_rows, even, odd, folded, gather, diag = refs[2 * QUARTERS :]
    atoms = c_ref.shape[0]
    targets = atoms * pairs_atom
    me = me_ref[0]

    @pl.when(pl.program_id(0) == 0)
    def _():
        shape = (targets, targets * NB)
        row, col = iota(shape, 0), iota(shape, 1)
        for r in range(QUARTERS):
            keep = (row == col // NB) & (((me + r) & 3) == (col % NB) // 8)
            gather[r * targets : (r + 1) * targets] = keep.astype(F32).astype(BF16)
        square = (WIDE, WIDE)
        diag[...] = (iota(square, 0) // NB == iota(square, 1) // NB).astype(F32).astype(BF16)

    lanes = WIDE // 2
    square = (lanes, lanes)
    fold = (iota(square, 0) % NB == iota(square, 1) % NB).astype(F32).astype(BF16)
    spread = (targets, 8, lanes)
    low = iota(spread, 2) // NB == iota(spread, 1)
    high = iota(spread, 2) // NB + 4 == iota(spread, 1)
    for r, y_ref in enumerate(y_refs):
        y_all[(me + r) & 3] = y_ref[...].astype(F32)
    parts = []
    for j in range(QUARTERS):
        y = y_all[j]
        left = jnp.broadcast_to(y[:, None, :lanes], spread)
        right = jnp.broadcast_to(y[:, None, lanes:], spread)
        parts.append(jnp.where(low, left, jnp.where(high, right, 0.0)))
    rows = jnp.concatenate(parts, axis=1).reshape(targets * NB, lanes).astype(BF16)
    rows = jnp.dot(rows, fold, preferred_element_type=F32).astype(BF16)
    y_rows[:, :lanes] = rows
    y_rows[:, lanes:] = rows
    tall = (pairs_atom * NB, WIDE)
    keep_out = iota(tall, 0) % 8 == iota(tall, 1) // NB

    halves = 2
    chunks = 8 // halves

    def first(a, t):
        target = a * pairs_atom + t
        y = y_rows[target * NB : (target + 1) * NB, :]
        y = jnp.concatenate([y] * 8, axis=0) * diag[...]
        inner = jnp.dot(c_ref[a], y, preferred_element_type=F32)
        inner = inner.reshape(8, NB, WIDE) * w_ref[target][:, None, :]
        inner = inner.astype(BF16)
        weighted = (even, odd)[a % 2]
        for p in range(8):
            weighted[t * NB : (t + 1) * NB, WIDE * p : WIDE * (p + 1)] = inner[p]

    def second(a, half):
        c = c_ref[a]
        chunk = range(half * chunks, (half + 1) * chunks)
        flat = jnp.concatenate([c[NB * p : NB * (p + 1), :] for p in chunk], axis=1)
        flat = jnp.concatenate([flat] * 8, axis=0)
        lanes_here = slice(half * chunks * WIDE, (half + 1) * chunks * WIDE)
        weighted = (even, odd)[a % 2][:, lanes_here]
        return lax.dot_general(weighted, flat, NT, preferred_element_type=F32)

    for a in range(atoms + 1):
        total = None
        for t in range(pairs_atom):
            if a < atoms:
                first(a, t)
            if a > 0 and (t + 1) % (pairs_atom // halves) == 0:
                part = second(a - 1, t // (pairs_atom // halves))
                total = part if total is None else total + part
        if a > 0:
            here = slice((a - 1) * pairs_atom * NB, a * pairs_atom * NB)
            folded[here] = jnp.where(keep_out, total, 0.0).astype(BF16)
    result = jnp.dot(gather[...], folded[...], preferred_element_type=F32).astype(BF16)
    for r, o_ref in enumerate(o_refs):
        o_ref[...] = result[r * targets : (r + 1) * targets]


def exchange(me, coeff, weights, quarters):
    atoms = coeff.shape[0]
    targets = weights.shape[0]
    pairs_atom = targets // atoms
    step = GROUP * pairs_atom
    part = pl.BlockSpec((step, WIDE), lambda i: (i, 0))

    def kernel(*refs):
        exchange_kernel(pairs_atom, *refs)

    return pl.pallas_call(
        kernel,
        grid=(atoms // GROUP,),
        in_specs=[
            pl.BlockSpec(memory_space=pltpu.SMEM),
            pl.BlockSpec((GROUP, WIDE, WIDE), lambda i: (i, 0, 0)),
            pl.BlockSpec((step, 8, WIDE), lambda i: (i, 0, 0)),
        ]
        + [part] * QUARTERS,
        out_specs=[part] * QUARTERS,
        out_shape=[jax.ShapeDtypeStruct((targets, WIDE), BF16)] * QUARTERS,
        scratch_shapes=[
            pltpu.VMEM((QUARTERS, step, WIDE), F32),
            pltpu.VMEM((step * NB, WIDE), BF16),
            pltpu.VMEM((pairs_atom * NB, 8 * WIDE), BF16),
            pltpu.VMEM((pairs_atom * NB, 8 * WIDE), BF16),
            pltpu.VMEM((step * NB, WIDE), BF16),
            pltpu.VMEM((QUARTERS * step, step * NB), BF16),
            pltpu.VMEM((WIDE, WIDE), BF16),
        ],
        compiler_params=pltpu.CompilerParams(vmem_limit_bytes=FULL),
    )(me, coeff, weights, *quarters)


def rank(mesh, k, p, a):
    return (k % mesh.shape["ka"] * mesh.shape["pair"] + p) * mesh.shape["aux"] + a % mesh.shape["aux"]


def first_groups(mesh):
    ka, pair, aux = (mesh.shape[n] for n in AXES)
    groups = []
    for p in range(pair):
        if p % 2 == 0:
            groups += [[rank(mesh, k, p, a) for k in range(ka)] for a in range(aux)]
        else:
            groups += [[rank(mesh, k, p, a) for a in range(aux)] for k in range(ka)]
    return groups


def second_shift(mesh, by):
    ka, pair, aux = (mesh.shape[n] for n in AXES)
    pairs = []
    for k in range(ka):
        for p in range(pair):
            for a in range(aux):
                to = rank(mesh, k, p, a + by) if p % 2 == 0 else rank(mesh, k + by, p, a)
                pairs.append((rank(mesh, k, p, a), to))
    return pairs


def along_aux(array, by):
    return lax.ppermute(array, "aux", [(i, (i + by) % QUARTERS) for i in range(QUARTERS)])


def make_shards(mesh):
    def shards(
        kpoint_grid,
        image_shift,
        density_k,
        coefficients,
        coulomb,
        send_rows,
        source_index,
        list_length,
    ):
        targets = coulomb.shape[0]
        slots = send_rows.shape[1] * send_rows.shape[2]
        aux = lax.axis_index("aux")

        terms = kpoint_terms(kpoint_grid, image_shift, density_k[0])
        terms, coulomb, source_index, list_length, send_rows = lax.optimization_barrier(
            (terms, coulomb, source_index, list_length, send_rows)
        )
        terms = lax.all_to_all(
            terms, AXES, split_axis=0, concat_axis=0, tiled=True, axis_index_groups=first_groups(mesh)
        )
        counts, weights = entry_counts(source_index, list_length, coulomb, targets + slots)
        rows_out = send_rows.reshape(slots, 1)
        terms, weights, counts, rows_out = lax.optimization_barrier(
            (terms, weights, counts, rows_out)
        )
        halves = half_sums(terms)
        parts = [halves[0]] + [
            lax.ppermute(halves[by], AXES, second_shift(mesh, by)) for by in (2, 1, 3)
        ]
        slab, sent = pick(rows_out, parts)
        sent, coefficients = lax.optimization_barrier((sent, coefficients))
        sent = sent.reshape(send_rows.shape[1], send_rows.shape[2], WIDE)
        got = lax.all_to_all(sent, ("ka", "pair"), split_axis=0, concat_axis=0, tiled=True)
        coeff = relay_coefficients(coefficients)
        got, coeff = lax.optimization_barrier((got, coeff))
        y = list_sums(counts, slab, got.reshape(slots, WIDE))
        far, right, left = along_aux(y, 2), along_aux(y, -1), along_aux(y, 1)
        own, a, b, c = exchange(aux.reshape(1).astype(jnp.int32), coeff, weights, (y, right, far, left))
        total = own.astype(F32) + along_aux(b, 2).astype(F32)
        total += along_aux(a, 1).astype(F32) + along_aux(c, 3).astype(F32)
        return total.astype(BF16)

    return shards


def solution(mesh):
    placed = (
        P(("ka", "aux"), None),
        P(None, None, "pair"),
        P(("ka", "aux"), None, "pair", None, None),
        P(("ka", "pair"), "aux", None),
        P(("ka", "pair"), "aux"),
        P(("ka", "pair"), None, None),
        P(("ka", "pair"), None),
        P(("ka", "pair")),
    )
    return jax.shard_map(
        make_shards(mesh),
        mesh=mesh,
        in_specs=placed,
        out_specs=P(("ka", "pair"), "aux"),
        check_vma=False,
    )
```

```python
import math

import jax
import jax.numpy as jnp
from jax import lax
from jax.experimental import pallas as pl
from jax.experimental.pallas import tpu as pltpu
from jax.sharding import PartitionSpec as P

NB = 32
NK = 16
WIDE = 256
ROWS = 128
GROUP = 4
QUARTERS = 4
FULL = 60 * 2**20
AXES = ("ka", "pair", "aux")
F32 = jnp.float32
BF16 = jnp.bfloat16
NT = (((1,), (1,)), ((), ()))
TN = (((0,), (0,)), ((), ()))


def iota(shape, dim):
    return lax.broadcasted_iota(jnp.int32, shape, dim)


def term_kernel(kp_ref, shift_ref, x_ref, o_ref, stage, sem):
    g = pl.program_id(0)
    rows, _, width = x_ref.shape
    turns = (
        kp_ref[0, 0] * (NK // 4) * shift_ref[0, pl.ds(g, 1)]
        + kp_ref[0, 1] * (NK // 2) * shift_ref[1, pl.ds(g, 1)]
        + kp_ref[0, 2] * (NK // 2) * shift_ref[2, pl.ds(g, 1)]
    ) & (NK - 1)
    angle = turns.astype(F32) * (2.0 * math.pi / NK)
    even, odd = jnp.cos(angle) / NK, jnp.sin(angle) / NK
    row, col = iota((2 * ROWS, ROWS), 0), iota((2 * ROWS, ROWS), 1)
    core = lax.axis_index("pair") % 2
    second = jnp.where(core == 0, lax.axis_index("aux"), lax.axis_index("ka"))
    pieces = width // WIDE

    def copy_out(slab, j):
        first = jnp.where(core == 0, slab, j)
        other = (jnp.where(core == 0, j, slab) - second) & 3
        return pltpu.make_async_copy(stage.at[slab, j], o_ref.at[first, other], sem.at[slab, j])

    for i in range(rows // ROWS):
        here = slice(i * ROWS, (i + 1) * ROWS)
        phase = jnp.where(
            row == 2 * col, even[:, here], jnp.where(row == 2 * col + 1, odd[:, here], 0.0)
        )
        high = phase.astype(BF16)
        low = (phase - high.astype(F32)).astype(BF16)
        both = jnp.concatenate([high, low], axis=1).T
        block = x_ref[here].reshape(2 * ROWS, width)
        term = jnp.dot(both, block, preferred_element_type=F32)
        term = (term[:ROWS] + term[ROWS:]).astype(BF16)
        for j in range(pieces):
            stage[g, j, here] = term[:, WIDE * j : WIDE * (j + 1)]
    for j in range(pieces):
        copy_out(g, j).start()

    @pl.when(g == stage.shape[0] - 1)
    def _():
        for slab in range(stage.shape[0]):
            for j in range(pieces):
                copy_out(slab, j).wait()


def kpoint_terms(kpoint, shift, block):
    slabs, rows = block.shape[:2]
    width = block.shape[-1]
    shape = (slabs, width // WIDE, rows, WIDE)
    return pl.pallas_call(
        term_kernel,
        grid=(slabs,),
        in_specs=[
            pl.BlockSpec(memory_space=pltpu.SMEM),
            pl.BlockSpec((3, slabs, rows), lambda g: (0, 0, 0)),
            pl.BlockSpec((rows, 2, width), lambda g: (g, 0, 0)),
        ],
        out_specs=pl.BlockSpec(memory_space=pl.ANY),
        out_shape=jax.ShapeDtypeStruct(shape, BF16),
        scratch_shapes=[pltpu.VMEM(shape, BF16), pltpu.SemaphoreType.DMA(shape[:2])],
        compiler_params=pltpu.CompilerParams(vmem_limit_bytes=FULL),
    )(kpoint, shift, block.reshape(slabs * rows, 2, width))


def half_sum_kernel(x_ref, *o_refs):
    for q, o_ref in enumerate(o_refs):
        total = x_ref[0, q].astype(F32)
        for f in range(1, x_ref.shape[0]):
            total += x_ref[f, q].astype(F32)
        o_ref[...] = total.astype(BF16)


def half_sums(terms):
    parts, others, rows, width = terms.shape
    step = rows // 3
    return pl.pallas_call(
        half_sum_kernel,
        grid=(rows // step,),
        in_specs=[pl.BlockSpec((parts, others, step, width), lambda i: (0, 0, i, 0))],
        out_specs=[pl.BlockSpec((step, width), lambda i: (i, 0))] * others,
        out_shape=[jax.ShapeDtypeStruct((rows, width), BF16)] * others,
        compiler_params=pltpu.CompilerParams(vmem_limit_bytes=20 * 2**20),
    )(terms)


def relay_kernel(x_ref, o_ref, wide, spread, place):
    lanes = WIDE // 2

    @pl.when(pl.program_id(0) == 0)
    def _():
        row, col = iota((lanes, WIDE), 0), iota((lanes, WIDE), 1)
        for p in range(8):
            keep = (row % NB == col % NB) & (col // NB == p)
            place[lanes * p : lanes * (p + 1)] = keep.astype(F32).astype(BF16)

    low = iota((8, lanes), 0) == iota((8, lanes), 1) // NB
    high = iota((8, lanes), 0) == iota((8, lanes), 1) // NB + 4
    for a in range(x_ref.shape[0]):
        wide[a] = x_ref[a].astype(F32)
        for p in range(8):
            rows = []
            for q in range(8):
                here = slice(8 * q + p, 8 * q + p + 1)
                for j in range(4):
                    left = wide[a, here, WIDE * j : WIDE * j + lanes]
                    right = wide[a, here, WIDE * j + lanes : WIDE * (j + 1)]
                    left = jnp.broadcast_to(left, (8, lanes))
                    right = jnp.broadcast_to(right, (8, lanes))
                    rows.append(jnp.where(low, left, jnp.where(high, right, 0.0)))
            rows = jnp.concatenate(rows, axis=0).astype(BF16)
            spread[a, :, lanes * p : lanes * (p + 1)] = rows
        o_ref[a] = jnp.dot(spread[a], place[...], preferred_element_type=F32).astype(BF16)


def relay_coefficients(coefficients):
    atoms, aux, width = coefficients.shape
    return pl.pallas_call(
        relay_kernel,
        grid=(atoms // GROUP,),
        in_specs=[pl.BlockSpec((GROUP, aux, width), lambda i: (i, 0, 0))],
        out_specs=pl.BlockSpec((GROUP, WIDE, WIDE), lambda i: (i, 0, 0)),
        out_shape=jax.ShapeDtypeStruct((atoms, WIDE, WIDE), BF16),
        scratch_shapes=[
            pltpu.VMEM((GROUP, aux, width), F32),
            pltpu.VMEM((GROUP, WIDE, 4 * WIDE), BF16),
            pltpu.VMEM((4 * WIDE, WIDE), BF16),
        ],
        compiler_params=pltpu.CompilerParams(vmem_limit_bytes=20 * 2**20),
    )(coefficients)


def count_kernel(src_ref, len_ref, coul_ref, s_ref, w_ref):
    coul = coul_ref[...]
    rows, aux = coul.shape
    high = coul.astype(BF16)
    rest = coul - high.astype(F32)
    middle = rest.astype(BF16)
    pieces = [high, middle, (rest - middle.astype(F32)).astype(BF16)]
    for p in range(aux // 8):
        keep = iota((aux, WIDE), 0) == 8 * p + iota((aux, WIDE), 1) // NB
        keep = keep.astype(F32).astype(BF16)
        spread = [jnp.dot(piece, keep, preferred_element_type=F32) for piece in pieces]
        w_ref[:, p, :] = (spread[0] + spread[1]) + spread[2]
    lanes = 128
    shape = (src_ref.shape[0], lanes)
    zero, one = jnp.zeros((), BF16), jnp.ones((), BF16)
    lane = iota(shape, 1).astype(F32).astype(BF16)
    blocks, hits = [], []
    for g in range(src_ref.shape[1]):
        index = jnp.where(g < len_ref[...], src_ref[:, g : g + 1], -lanes)
        blocks.append(jnp.broadcast_to(index >> 7, shape).astype(F32).astype(BF16))
        within = jnp.broadcast_to(index & (lanes - 1), shape).astype(F32).astype(BF16)
        hits.append(jnp.where(within == lane, one, zero))
    for b in range(s_ref.shape[1] // lanes):
        here = jnp.full(shape, b, F32).astype(BF16)
        total = jnp.zeros(shape, BF16)
        for block, hit in zip(blocks, hits):
            total = total + jnp.where(block == here, hit, zero)
        s_ref[:, lanes * b : lanes * (b + 1)] = total


def entry_counts(source_index, list_length, coulomb, pool):
    targets, entries = source_index.shape
    aux = coulomb.shape[1]
    step = 64
    return pl.pallas_call(
        count_kernel,
        grid=(targets // step,),
        in_specs=[
            pl.BlockSpec((step, entries), lambda i: (i, 0)),
            pl.BlockSpec((step, 1), lambda i: (i, 0)),
            pl.BlockSpec((step, aux), lambda i: (i, 0)),
        ],
        out_specs=[
            pl.BlockSpec((step, pool), lambda i: (i, 0)),
            pl.BlockSpec((step, aux // 8, WIDE), lambda i: (i, 0, 0)),
        ],
        out_shape=[
            jax.ShapeDtypeStruct((targets, pool), BF16),
            jax.ShapeDtypeStruct((targets, aux // 8, WIDE), F32),
        ],
    )(source_index, list_length[:, None], coulomb)


def pick_kernel(rows_ref, own_ref, a_ref, b_ref, c_ref, slab_ref, sent_ref):
    total = own_ref[...].astype(F32) + a_ref[...].astype(F32)
    total += b_ref[...].astype(F32) + c_ref[...].astype(F32)
    slab = total.astype(BF16)
    slab_ref[...] = slab
    step = 256
    for i in range(sent_ref.shape[0] // step):
        rows = rows_ref[i * step : (i + 1) * step]
        hot = (rows == iota((step, slab.shape[0]), 1)).astype(F32).astype(BF16)
        sent_ref[i * step : (i + 1) * step] = jnp.dot(
            hot, slab, preferred_element_type=F32
        ).astype(BF16)


def pick(rows, parts):
    shape = parts[0].shape
    return pl.pallas_call(
        pick_kernel,
        out_shape=(
            jax.ShapeDtypeStruct(shape, BF16),
            jax.ShapeDtypeStruct((rows.shape[0], shape[1]), BF16),
        ),
        compiler_params=pltpu.CompilerParams(vmem_limit_bytes=12 * 2**20),
    )(rows, *parts)


def list_kernel(counts_ref, slab_ref, got_ref, y_ref):
    own = slab_ref.shape[0]
    total = jnp.dot(counts_ref[:, :own], slab_ref[...], preferred_element_type=F32)
    total += jnp.dot(counts_ref[:, own:], got_ref[...], preferred_element_type=F32)
    y_ref[...] = total.astype(BF16)


def list_sums(counts, slab, got):
    return pl.pallas_call(
        list_kernel,
        out_shape=jax.ShapeDtypeStruct((counts.shape[0], slab.shape[1]), BF16),
        compiler_params=pltpu.CompilerParams(vmem_limit_bytes=12 * 2**20),
    )(counts, slab, got)


def exchange_kernel(pairs_atom, me_ref, c_ref, w_ref, *refs):
    y_refs, o_refs = refs[:QUARTERS], refs[QUARTERS : 2 * QUARTERS]
    y_all, y_rows, even, odd, folded, gather, diag = refs[2 * QUARTERS :]
    atoms = c_ref.shape[0]
    targets = atoms * pairs_atom
    me = me_ref[0]

    @pl.when(pl.program_id(0) == 0)
    def _():
        shape = (targets, targets * NB)
        row, col = iota(shape, 0), iota(shape, 1)
        for r in range(QUARTERS):
            keep = (row == col // NB) & (((me + r) & 3) == (col % NB) // 8)
            gather[r * targets : (r + 1) * targets] = keep.astype(F32).astype(BF16)
        square = (WIDE, WIDE)
        diag[...] = (iota(square, 0) // NB == iota(square, 1) // NB).astype(F32).astype(BF16)

    lanes = WIDE // 2
    square = (lanes, lanes)
    fold = (iota(square, 0) % NB == iota(square, 1) % NB).astype(F32).astype(BF16)
    spread = (targets, 8, lanes)
    low = iota(spread, 2) // NB == iota(spread, 1)
    high = iota(spread, 2) // NB + 4 == iota(spread, 1)
    for ahead, y_ref in zip((0, 1, 3, 2), y_refs):
        y_all[(me + ahead) & 3] = y_ref[...].astype(F32)
    parts = []
    for j in range(QUARTERS):
        y = y_all[j]
        left = jnp.broadcast_to(y[:, None, :lanes], spread)
        right = jnp.broadcast_to(y[:, None, lanes:], spread)
        parts.append(jnp.where(low, left, jnp.where(high, right, 0.0)))
    rows = jnp.concatenate(parts, axis=1).reshape(targets * NB, lanes).astype(BF16)
    rows = jnp.dot(rows, fold, preferred_element_type=F32).astype(BF16)
    y_rows[:, :lanes] = rows
    y_rows[:, lanes:] = rows
    tall = (pairs_atom * NB, WIDE)
    keep_out = iota(tall, 0) % 8 == iota(tall, 1) // NB

    halves = 2
    chunks = 8 // halves

    def first(a, t):
        target = a * pairs_atom + t
        y = y_rows[target * NB : (target + 1) * NB, :]
        y = jnp.concatenate([y] * 8, axis=0) * diag[...]
        inner = jnp.dot(c_ref[a], y, preferred_element_type=F32)
        inner = inner.reshape(8, NB, WIDE) * w_ref[target][:, None, :]
        inner = inner.astype(BF16)
        weighted = (even, odd)[a % 2]
        for p in range(8):
            weighted[t * NB : (t + 1) * NB, WIDE * p : WIDE * (p + 1)] = inner[p]

    def second(a, half):
        c = c_ref[a]
        chunk = range(half * chunks, (half + 1) * chunks)
        flat = jnp.concatenate([c[NB * p : NB * (p + 1), :] for p in chunk], axis=1)
        flat = jnp.concatenate([flat] * 8, axis=0)
        lanes_here = slice(half * chunks * WIDE, (half + 1) * chunks * WIDE)
        weighted = (even, odd)[a % 2][:, lanes_here]
        return lax.dot_general(weighted, flat, NT, preferred_element_type=F32)

    for a in range(atoms + 1):
        total = None
        for t in range(pairs_atom):
            if a < atoms:
                first(a, t)
            if a > 0 and (t + 1) % (pairs_atom // halves) == 0:
                part = second(a - 1, t // (pairs_atom // halves))
                total = part if total is None else total + part
        if a > 0:
            here = slice((a - 1) * pairs_atom * NB, a * pairs_atom * NB)
            folded[here] = jnp.where(keep_out, total, 0.0).astype(BF16)
    result = jnp.dot(gather[...], folded[...], preferred_element_type=F32).astype(BF16)
    for r, o_ref in enumerate(o_refs):
        o_ref[...] = result[r * targets : (r + 1) * targets]


def exchange(me, coeff, weights, quarters):
    atoms = coeff.shape[0]
    targets = weights.shape[0]
    pairs_atom = targets // atoms
    step = GROUP * pairs_atom
    part = pl.BlockSpec((step, WIDE), lambda i: (i, 0))

    def kernel(*refs):
        exchange_kernel(pairs_atom, *refs)

    return pl.pallas_call(
        kernel,
        grid=(atoms // GROUP,),
        in_specs=[
            pl.BlockSpec(memory_space=pltpu.SMEM),
            pl.BlockSpec((GROUP, WIDE, WIDE), lambda i: (i, 0, 0)),
            pl.BlockSpec((step, 8, WIDE), lambda i: (i, 0, 0)),
        ]
        + [part] * QUARTERS,
        out_specs=[part] * QUARTERS,
        out_shape=[jax.ShapeDtypeStruct((targets, WIDE), BF16)] * QUARTERS,
        scratch_shapes=[
            pltpu.VMEM((QUARTERS, step, WIDE), F32),
            pltpu.VMEM((step * NB, WIDE), BF16),
            pltpu.VMEM((pairs_atom * NB, 8 * WIDE), BF16),
            pltpu.VMEM((pairs_atom * NB, 8 * WIDE), BF16),
            pltpu.VMEM((step * NB, WIDE), BF16),
            pltpu.VMEM((QUARTERS * step, step * NB), BF16),
            pltpu.VMEM((WIDE, WIDE), BF16),
        ],
        compiler_params=pltpu.CompilerParams(vmem_limit_bytes=FULL),
    )(me, coeff, weights, *quarters)


def rank(mesh, k, p, a):
    return (k % mesh.shape["ka"] * mesh.shape["pair"] + p) * mesh.shape["aux"] + a % mesh.shape["aux"]


def first_groups(mesh):
    ka, pair, aux = (mesh.shape[n] for n in AXES)
    groups = []
    for p in range(pair):
        if p % 2 == 0:
            groups += [[rank(mesh, k, p, a) for k in range(ka)] for a in range(aux)]
        else:
            groups += [[rank(mesh, k, p, a) for a in range(aux)] for k in range(ka)]
    return groups


def second_shift(mesh, by):
    ka, pair, aux = (mesh.shape[n] for n in AXES)
    pairs = []
    for k in range(ka):
        for p in range(pair):
            for a in range(aux):
                to = rank(mesh, k, p, a + by) if p % 2 == 0 else rank(mesh, k + by, p, a)
                pairs.append((rank(mesh, k, p, a), to))
    return pairs


def along_aux(array, by):
    return lax.ppermute(array, "aux", [(i, (i + by) % QUARTERS) for i in range(QUARTERS)])


def make_shards(mesh):
    def shards(
        kpoint_grid,
        image_shift,
        density_k,
        coefficients,
        coulomb,
        send_rows,
        source_index,
        list_length,
    ):
        targets = coulomb.shape[0]
        slots = send_rows.shape[1] * send_rows.shape[2]
        aux = lax.axis_index("aux")

        terms = kpoint_terms(kpoint_grid, image_shift, density_k[0])
        terms, coulomb, source_index, list_length, send_rows = lax.optimization_barrier(
            (terms, coulomb, source_index, list_length, send_rows)
        )
        terms = lax.all_to_all(
            terms, AXES, split_axis=0, concat_axis=0, tiled=True, axis_index_groups=first_groups(mesh)
        )
        counts, weights = entry_counts(source_index, list_length, coulomb, targets + slots)
        rows_out = send_rows.reshape(slots, 1)
        terms, weights, counts, rows_out = lax.optimization_barrier(
            (terms, weights, counts, rows_out)
        )
        halves = half_sums(terms)
        parts = [halves[0]] + [
            lax.ppermute(halves[by], AXES, second_shift(mesh, by)) for by in (2, 1, 3)
        ]
        slab, sent = pick(rows_out, parts)
        sent, coefficients = lax.optimization_barrier((sent, coefficients))
        sent = sent.reshape(send_rows.shape[1], send_rows.shape[2], WIDE)
        got = lax.all_to_all(sent, ("ka", "pair"), split_axis=0, concat_axis=0, tiled=True)
        coeff = relay_coefficients(coefficients)
        got, coeff = lax.optimization_barrier((got, coeff))
        y = list_sums(counts, slab, got.reshape(slots, WIDE))
        far, right, left = along_aux(y, 2), along_aux(y, -1), along_aux(y, 1)
        own, a, b, c = exchange(aux.reshape(1).astype(jnp.int32), coeff, weights, (y, right, left, far))
        total = own.astype(F32) + along_aux(b, 2).astype(F32)
        total += along_aux(a, 1).astype(F32) + along_aux(c, 3).astype(F32)
        return total.astype(BF16)

    return shards


def solution(mesh):
    placed = (
        P(("ka", "aux"), None),
        P(None, None, "pair"),
        P(("ka", "aux"), None, "pair", None, None),
        P(("ka", "pair"), "aux", None),
        P(("ka", "pair"), "aux"),
        P(("ka", "pair"), None, None),
        P(("ka", "pair"), None),
        P(("ka", "pair")),
    )
    return jax.shard_map(
        make_shards(mesh),
        mesh=mesh,
        in_specs=placed,
        out_specs=P(("ka", "pair"), "aux"),
        check_vma=False,
    )
```
